32 devices in a mesh: groups: 2 (over y), layer: 4 (over z), latent: 4 (over x, core).
Axes of the slice: x: 2, y: 2, z: 4, core: 2. Of those that a mesh axis runs over, the one named last changes fastest.
Arguments:
- acts: bfloat16 [2048, 14336], P('groups', 'layer'), parts along dimension 0, may hold values from -96 to 96, as said below
- enc_weight: bfloat16 [14336, 8192], P('layer', ('groups', 'latent')), parts along dimension 1, may hold values from -0.046875 to 0.046875
- dec_weight: bfloat16 [8192, 14336], P(('groups', 'latent'), 'layer'), parts along dimension 0, may hold values from -0.09375 to 0.09375
- enc_bias: float32 [8192], P(('groups', 'latent')), parts along dimension 0, may hold values from -4 to 4
- dec_bias: float32 [28672], P(('groups', 'layer')), parts along dimension 0, may hold values from -3 to 3
Outputs:
- grad_enc: bfloat16 [14336, 8192], P('layer', ('groups', 'latent')), parts along dimension 1
- grad_dec: bfloat16 [8192, 14336], P(('groups', 'latent'), 'layer'), parts along dimension 0
- grad_benc: float32 [8192], P(('groups', 'latent')), parts along dimension 0
- grad_bdec: float32 [28672], P(('groups', 'layer')), parts along dimension 0
- loss: float32 [2], P('groups'), parts along dimension 0
The draws below stay inside these ranges and needn't reach their ends.
There are 2 independent parts, one for each index of `groups`. The reference program is written for one: setup_inputs(seed, part) draws one part's arguments, and reference() takes and returns one part's arrays. A program takes and returns all parts, laid end to end along the dimension named above; each array names one. Nothing has to cross between parts.
Inputs may be any that keep to these rules, and one draw needn't show every extreme that they name: `acts`: residual activations; their scale differs between tokens, features and layers.
All inputs are finite; a program needn't handle non-finite values.
Results may differ from the reference program's by a relative error of at most 0.0056.
Values may be sent and summed in bfloat16 or wider, within the bound.
A program may use at most 192 MiB of HBM per device.

```python
import math
import jax
import jax.numpy as jnp
from jax import lax

D = 3584
LAYERS = 4
TOKENS = 1024
FEATURES = 14336
LATENTS = 4096


def draw_acts(key, part):
    key = jax.random.fold_in(key, 11)
    first, second, third = jax.random.split(key, 3)
    base = jnp.clip(jax.random.normal(first, (TOKENS, LAYERS, D), jnp.float32), -4.0, 4.0)
    depth = 1.0 + 2.0 * jnp.arange(LAYERS, dtype=jnp.float32) / max(LAYERS - 1, 1)
    row_scale = jnp.exp(jax.random.uniform(second, (TOKENS, 1, 1), jnp.float32, math.log(0.4), math.log(4.0)))
    col_scale = jnp.exp(jax.random.uniform(third, (1, 1, D), jnp.float32, math.log(0.5), math.log(2.0)))
    values = base * depth[None, :, None] * row_scale * col_scale
    return values.reshape(TOKENS, LAYERS * D).astype(jnp.bfloat16)


def steps_of(key, dims, cuts, smallest, top_value):
    loudness = 1.0
    for axis_at, parts in cuts:
        heights = jax.random.uniform(jax.random.fold_in(jax.random.fold_in(key, 6), axis_at), (parts,), jnp.float32, smallest / len(cuts), top_value / len(cuts))
        loudness = loudness * jnp.repeat(jnp.exp(heights), dims[axis_at] // parts).reshape((-1,) + (1,) * (len(dims) - 1 - axis_at))
    return loudness


def centred(key, extent, spread, most, cuts=(), held_as=jnp.bfloat16):
    drawn = jax.random.normal(key, extent, jnp.float32) * spread
    if len(cuts) > 0:
        drawn = steps_of(key, extent, cuts, -0.22, 0.18) * drawn
    return jnp.clip(drawn, min=-most, max=most).astype(held_as)


def setup_inputs(seed: int = 0, part: int = 0) -> dict:
    keys = jax.random.split(jax.random.key(seed), 6)
    own_keys = jax.random.split(jax.random.fold_in(keys[5], part), 6)
    return {
        "acts": draw_acts(jax.random.fold_in(jax.random.fold_in(keys[5], part), 71), part),
        "enc_weight": centred(own_keys[1], (FEATURES, LATENTS), FEATURES ** -0.5, 0.046875, ((0, 4), (1, 4))),
        "dec_weight": centred(own_keys[2], (LATENTS, FEATURES), LATENTS ** -0.5, 0.09375, ((0, 4), (1, 4))),
        "enc_bias": centred(own_keys[3], (LATENTS,), 1.0, 4.0, ((0, 4),), jnp.float32),
        "dec_bias": centred(own_keys[4], (FEATURES,), 0.5, 3.0, ((0, 4),), jnp.float32),
    }


def reference(acts, enc_weight, dec_weight, enc_bias, dec_bias):
    pre = jnp.dot(acts, enc_weight, preferred_element_type=jnp.float32) + enc_bias
    feats = jnp.maximum(pre, 0.0).astype(jnp.bfloat16)
    dec_wide = dec_weight.astype(jnp.float32).reshape(LATENTS, LAYERS, D)
    norms = jnp.sqrt(lax.optimization_barrier(jnp.sum(dec_wide * dec_wide, axis=2)) + 1e-06)
    weight = lax.optimization_barrier(jnp.sum(norms, axis=1))
    recon = jnp.dot(feats, dec_weight, preferred_element_type=jnp.float32) + dec_bias
    error = recon - acts.astype(jnp.float32)
    feats_wide = feats.astype(jnp.float32)
    total = jnp.sum(error * error) + 4.0 * jnp.sum(feats_wide * weight[None, :])
    loss = (total / (TOKENS * FEATURES)).reshape(1)
    grad_error = (2.0 / TOKENS * error).astype(jnp.bfloat16)
    grad_bdec = lax.optimization_barrier(jnp.sum(grad_error.astype(jnp.float32), axis=0))
    feat_total = lax.optimization_barrier(jnp.sum(feats_wide, axis=0))
    outer = lax.dot_general(feats, grad_error, (((0,), (0,)), ((), ())), preferred_element_type=jnp.float32)
    scaled = (dec_wide / norms[:, :, None]).reshape(LATENTS, FEATURES)
    grad_dec = (outer + 4.0 / TOKENS * feat_total[:, None] * scaled).astype(jnp.bfloat16)
    grad_feats = lax.dot_general(grad_error, dec_weight, (((1,), (1,)), ((), ())), preferred_element_type=jnp.float32)
    grad_feats = grad_feats + 4.0 / TOKENS * weight[None, :]
    grad_pre = jnp.where(feats > 0, grad_feats, 0.0).astype(jnp.bfloat16)
    grad_benc = lax.optimization_barrier(jnp.sum(grad_pre.astype(jnp.float32), axis=0))
    grad_enc = lax.dot_general(acts, grad_pre, (((0,), (0,)), ((), ())), preferred_element_type=jnp.float32).astype(jnp.bfloat16)
    return (grad_enc, grad_dec, grad_benc, grad_bdec, loss)
```

```python
import functools

import jax
import jax.numpy as jnp
from jax import lax
from jax.experimental import pallas as pl
from jax.experimental.pallas import tpu as pltpu
from jax.sharding import PartitionSpec as P

D = 3584
LAYERS = 4
PIECE = 128
MESH = pl.DeviceIdType.MESH
F32 = jnp.float32
BF16 = jnp.bfloat16


def tokens_kernel(
    layer_count, acts_h, enc_h, dec_h, ebias, dbias, norms_in,
    feats_h, gerr_h, gpre_h, mse, wsum,
    enc_v, dec_v, acts_a, acts_e, part, pre_in, feats, out_half, own_half, core_in, x_in,
    gerr, gpart, g_in, gpre, norms_all,
    load_sem, acts_sem, acte_sem, store_sem, norm_send, norm_recv,
    ps, pr, fs, fr, cs, cr, xs, xr, es, er, gs, gr, bs, br,
):
    tok_rows, width = acts_h.shape
    lat = enc_h.shape[1]
    T = PIECE
    H = T // 2
    NP = tok_rows // T
    last = layer_count - 1
    grp, z, k = lax.axis_index("groups"), lax.axis_index("layer"), lax.axis_index("latent")
    core = k % 2
    mate = (grp, z, k + 1 - 2 * core)
    across = (grp, z, (k + 2) % 4)

    def level(i):
        return (grp, i, k)

    enc_load = pltpu.make_async_copy(enc_h, enc_v, load_sem.at[0])
    dec_load = pltpu.make_async_copy(dec_h, dec_v, load_sem.at[1])

    def acts_load(p):
        return pltpu.make_async_copy(
            acts_h.at[pl.ds(p * T, T)], acts_a.at[p % 2], acts_sem.at[p % 2]
        )

    def acte_load(p):
        return pltpu.make_async_copy(
            acts_h.at[pl.ds(p * T + core * H, H)], acts_e.at[p % 2], acte_sem.at[p % 2]
        )

    enc_load.start()
    acts_load(0).start()
    dec_load.start()
    mse[...] = jnp.zeros_like(mse)

    barrier = pltpu.get_barrier_semaphore()
    for step in range(1, layer_count):
        pl.semaphore_signal(
            barrier, inc=1, device_id=level((z + step) % layer_count), device_id_type=MESH
        )
    pl.semaphore_signal(barrier, inc=1, device_id=mate, device_id_type=MESH)
    pl.semaphore_signal(barrier, inc=1, device_id=across, device_id_type=MESH)
    pl.semaphore_wait(barrier, layer_count + 1)

    def remote(src, dst, send, recv, dev):
        return pltpu.make_async_remote_copy(
            src_ref=src, dst_ref=dst, send_sem=send, recv_sem=recv,
            device_id=dev, device_id_type=MESH,
        )

    def norm_copy(step):
        return remote(
            norms_in, norms_all.at[step], norm_send.at[step], norm_recv.at[step],
            level((z + step) % layer_count),
        )

    for step in range(1, layer_count):
        norm_copy(step).start()

    def half_rows(way, p):
        return pl.ds(pl.multiple_of(p * T + way * H, H), H)

    def pos_of(way):
        return z if way == 0 else last - z

    def onward(way, by):
        nxt = z + by if way == 0 else z - by
        return level(jnp.clip(nxt, 0, last))

    def pre_copy(way, p):
        return remote(part.at[half_rows(way, p)], pre_in.at[half_rows(way, p)],
                      ps.at[way, p], pr.at[way, p], onward(way, 1))

    def feat_copy(way, p):
        return remote(feats.at[half_rows(way, p)], feats.at[half_rows(way, p)],
                      fs.at[way, p], fr.at[way, p], onward(way, -1))

    def grad_copy(way, p):
        return remote(gpart.at[half_rows(way, p)], g_in.at[half_rows(way, p)],
                      gs.at[way, p], gr.at[way, p], onward(way, 1))

    def gpre_copy(way, p):
        return remote(gpre.at[half_rows(way, p)], gpre.at[half_rows(way, p)],
                      bs.at[way, p], br.at[way, p], onward(way, -1))

    def half_of(p):
        return pl.ds(pl.multiple_of(p * H, H), H)

    def core_copy(p):
        return remote(out_half.at[half_of(p)], core_in.at[half_of(p)], cs.at[p], cr.at[p], mate)

    def x_copy(p):
        return remote(own_half.at[half_of(p)], x_in.at[half_of(p)], xs.at[p], xr.at[p], across)

    def err_copy(p):
        rows = pl.ds(pl.multiple_of(p * T + core * H, H), H)
        return remote(gerr.at[rows], gerr.at[rows], es.at[p], er.at[p], mate)

    def piece_rows(p):
        return pl.ds(pl.multiple_of(p * T, T), T)

    def store(which, p):
        src, dst = ((feats, feats_h), (gerr, gerr_h), (gpre, gpre_h))[which]
        return pltpu.make_async_copy(
            src.at[piece_rows(p)], dst.at[piece_rows(p)], store_sem.at[which, p]
        )

    def valid(p):
        return jnp.logical_and(p >= 0, p < NP)

    def pre_chain(t, first):
        for way in range(2):
            pos = pos_of(way)
            p = t - pos
            here = pos == 0 if first else pos > 0

            @pl.when(jnp.logical_and(valid(p), here))
            def _():
                rows = half_rows(way, p)
                if not first:
                    pre_copy(way, p).wait_recv()

                    @pl.loop(0, lat // 256)
                    def _(n):
                        cols = pl.ds(pl.multiple_of(n * 256, 256), 256)
                        part[rows, cols] += pre_in[rows, cols]

                    @pl.when(pos < last)
                    def _():
                        pre_copy(way, p).start()

                    @pl.when(pos == last)
                    def _():
                        @pl.loop(0, lat // 256)
                        def _(n):
                            cols = pl.ds(pl.multiple_of(n * 256, 256), 256)
                            feats[rows, cols] = jnp.maximum(
                                part[rows, cols] + ebias[:, cols], 0.0
                            ).astype(BF16)
                        feat_copy(way, p).start()
                else:
                    pre_copy(way, p).start()

    def grad_chain(t, first):
        for way in range(2):
            pos = pos_of(way)
            p = t - pos
            here = pos == 0 if first else pos > 0

            @pl.when(jnp.logical_and(valid(p), here))
            def _():
                rows = half_rows(way, p)
                if not first:
                    grad_copy(way, p).wait_recv()

                    @pl.when(pos < last)
                    def _():
                        @pl.loop(0, lat // 256)
                        def _(n):
                            cols = pl.ds(pl.multiple_of(n * 256, 256), 256)
                            gpart[rows, cols] = (
                                gpart[rows, cols].astype(F32) + g_in[rows, cols].astype(F32)
                            ).astype(BF16)
                        grad_copy(way, p).start()

                    @pl.when(pos == last)
                    def _():
                        @pl.loop(0, lat // 256)
                        def _(n):
                            cols = pl.ds(pl.multiple_of(n * 256, 256), 256)
                            total = (
                                gpart[rows, cols].astype(F32)
                                + g_in[rows, cols].astype(F32)
                                + 4.0 / tok_rows * wsum[0:1, cols]
                            )
                            live = feats[rows, cols].astype(F32) > 0.0
                            gpre[rows, cols] = jnp.where(live, total, 0.0).astype(BF16)
                        gpre_copy(way, p).start()
                else:
                    grad_copy(way, p).start()

    def back(t, copy):
        for way in range(2):
            pos = pos_of(way)
            p = t - (2 * last - pos)

            @pl.when(jnp.logical_and(valid(p), pos < last))
            def _():
                copy(way, p).wait_recv()

                @pl.when(pos > 0)
                def _():
                    copy(way, p).start()

    enc_load.wait()
    LR = 2 * last + 1
    LC, LX, LG = LR + 1, LR + 2, LR + 3

    @pl.loop(0, NP + LG + 2 * last + 1)
    def _(t):
        @pl.when(t == LR)
        def _():
            dec_load.wait()
            total = norms_in[...]
            for step in range(1, layer_count):
                norm_copy(step).wait_recv()
                total = total + norms_all[step]
            wsum[...] = total

        back(t - LG, gpre_copy)
        p_done = t - LG - 2 * last

        @pl.when(valid(p_done))
        def _():
            store(2, p_done).start()

        grad_chain(t - LG, False)
        back(t, feat_copy)
        pre_chain(t, False)

        p_x = t - LX

        @pl.when(valid(p_x))
        def _():
            x_copy(p_x).wait_recv()
            acte_load(p_x).wait()
            rows = half_of(p_x)
            grows = pl.ds(pl.multiple_of(p_x * T + core * H, H), H)

            @pl.loop(0, width // 256)
            def _(n):
                cols = pl.ds(pl.multiple_of(n * 256, 256), 256)
                error = (
                    own_half[rows, cols].astype(F32) + x_in[rows, cols].astype(F32)
                    + dbias[:, cols] - acts_e[p_x % 2, :, cols].astype(F32)
                )
                mse[:, cols] += jnp.sum((error * error).reshape(H // 8, 8, 256), axis=0)
                gerr[grows, cols] = (2.0 / tok_rows * error).astype(BF16)
            err_copy(p_x).start()

        p_c = t - LC

        @pl.when(valid(p_c))
        def _():
            acte_load(p_c).start()
            core_copy(p_c).wait_recv()
            rows = half_of(p_c)

            @pl.loop(0, width // 256)
            def _(n):
                cols = pl.ds(pl.multiple_of(n * 256, 256), 256)
                own_half[rows, cols] = (
                    own_half[rows, cols].astype(F32) + core_in[rows, cols].astype(F32)
                ).astype(BF16)
            x_copy(p_c).start()

        @pl.when(t < NP)
        def _():
            acts_load(t).wait()

            @pl.when(t + 1 < NP)
            def _():
                acts_load(t + 1).start()

            rows = piece_rows(t)

            @pl.loop(0, lat // 256)
            def _(n):
                cols = pl.ds(pl.multiple_of(n * 256, 256), 256)
                part[rows, cols] = jnp.dot(
                    acts_a[t % 2], enc_v[:, cols], preferred_element_type=F32
                )
        pre_chain(t, True)

        p_r = t - LR

        @pl.when(valid(p_r))
        def _():
            store(0, p_r).start()
            mine = pl.ds(pl.multiple_of(p_r * T + core * H, H), H)
            other = pl.ds(pl.multiple_of(p_r * T + (1 - core) * H, H), H)
            rows = half_of(p_r)

            @pl.loop(0, width // 512)
            def _(n):
                cols = pl.ds(pl.multiple_of(n * 512, 512), 512)
                both = jnp.concatenate([feats[mine, :], feats[other, :]], axis=0)
                made = jnp.dot(both, dec_v[:, cols], preferred_element_type=F32)
                own_half[rows, cols] = made[:H].astype(BF16)
                out_half[rows, cols] = made[H:].astype(BF16)
            core_copy(p_r).start()

        p_g = t - LG

        @pl.when(valid(p_g))
        def _():
            err_copy(p_g).wait_recv()
            store(1, p_g).start()
            rows = piece_rows(p_g)

            @pl.loop(0, lat // 256)
            def _(n):
                cols = pl.ds(pl.multiple_of(n * 256, 256), 256)
                gpart[rows, cols] = lax.dot_general(
                    gerr[rows, :], dec_v[cols, :], (((1,), (1,)), ((), ())),
                    preferred_element_type=F32,
                ).astype(BF16)
        grad_chain(t - LG, True)

    for step in range(1, layer_count):
        norm_copy(step).wait_send()

    @pl.loop(0, NP)
    def _(p):
        for which in range(3):
            store(which, p).wait()
        core_copy(p).wait_send()
        x_copy(p).wait_send()
        err_copy(p).wait_send()
        for way in range(2):
            pos = pos_of(way)

            @pl.when(pos < last)
            def _():
                pre_copy(way, p).wait_send()
                grad_copy(way, p).wait_send()

            @pl.when(pos > 0)
            def _():
                feat_copy(way, p).wait_send()
                gpre_copy(way, p).wait_send()


def on_device_kernel(acts, enc_weight, dec_weight, enc_bias, dec_bias):
    tok_rows, width = acts.shape
    lat = enc_weight.shape[1]
    layer_count = lax.axis_size("layer")
    dec_wide = dec_weight.astype(F32)
    norms = jnp.sqrt(jnp.sum(dec_wide * dec_wide, axis=1) + 1e-06)
    half = tok_rows // 2
    pieces = tok_rows // PIECE
    dma = pltpu.SemaphoreType.DMA
    vm = pl.BlockSpec(memory_space=pltpu.VMEM)
    hb = pl.BlockSpec(memory_space=pl.ANY)
    feats, grad_error, grad_pre, mse, wsum = pl.pallas_call(
        functools.partial(tokens_kernel, layer_count),
        out_shape=(
            jax.ShapeDtypeStruct((tok_rows, lat), BF16),
            jax.ShapeDtypeStruct((tok_rows, width), BF16),
            jax.ShapeDtypeStruct((tok_rows, lat), BF16),
            jax.ShapeDtypeStruct((8, width), F32),
            jax.ShapeDtypeStruct((8, lat), F32),
        ),
        in_specs=[hb, hb, hb, vm, vm, vm],
        out_specs=(hb, hb, hb, vm, vm),
        scratch_shapes=[
            pltpu.VMEM((width, lat), BF16),
            pltpu.VMEM((lat, width), BF16),
            pltpu.VMEM((2, PIECE, width), BF16),
            pltpu.VMEM((2, PIECE // 2, width), BF16),
            pltpu.VMEM((tok_rows, lat), F32),
            pltpu.VMEM((tok_rows, lat), F32),
            pltpu.VMEM((tok_rows, lat), BF16),
            pltpu.VMEM((half, width), BF16),
            pltpu.VMEM((half, width), BF16),
            pltpu.VMEM((half, width), BF16),
            pltpu.VMEM((half, width), BF16),
            pltpu.VMEM((tok_rows, width), BF16),
            pltpu.VMEM((tok_rows, lat), BF16),
            pltpu.VMEM((tok_rows, lat), BF16),
            pltpu.VMEM((tok_rows, lat), BF16),
            pltpu.VMEM((layer_count, 8, lat), F32),
            dma((2,)), dma((2,)), dma((2,)), dma((3, pieces)),
            dma((layer_count,)), dma((layer_count,)),
            dma((2, pieces)), dma((2, pieces)), dma((2, pieces)), dma((2, pieces)),
            dma((pieces,)), dma((pieces,)), dma((pieces,)), dma((pieces,)),
            dma((pieces,)), dma((pieces,)),
            dma((2, pieces)), dma((2, pieces)), dma((2, pieces)), dma((2, pieces)),
        ],
        compiler_params=pltpu.CompilerParams(
            collective_id=0, has_side_effects=True, vmem_limit_bytes=62 * 1024 * 1024
        ),
        cost_estimate=pl.CostEstimate(
            flops=6 * tok_rows * width * lat, bytes_accessed=8 * tok_rows * width, transcendentals=0
        ),
    )(
        acts, enc_weight, dec_weight, enc_bias.reshape(1, lat), dec_bias.reshape(1, width),
        jnp.broadcast_to(norms[None, :], (8, lat)),
    )
    feat_total = jnp.sum(feats.astype(F32), axis=0)
    sparse_local = jnp.sum(feat_total * wsum[0])
    totals = lax.psum(jnp.stack([jnp.sum(mse), sparse_local]), ("layer", "latent"))
    total = totals[0] / 2 + 4.0 * totals[1] / layer_count
    loss = (total / (tok_rows * LAYERS * D)).reshape(1)
    grad_bdec = jnp.sum(grad_error.astype(F32), axis=0)
    outer = lax.dot_general(
        feats, grad_error, (((0,), (0,)), ((), ())), preferred_element_type=F32
    )
    coef = 4.0 / tok_rows * feat_total / norms
    grad_dec = (outer + coef[:, None] * dec_wide).astype(BF16)
    grad_benc = jnp.sum(grad_pre.astype(F32), axis=0)
    grad_enc = lax.dot_general(
        acts, grad_pre, (((0,), (0,)), ((), ())), preferred_element_type=F32
    ).astype(BF16)
    return (grad_enc, grad_dec, grad_benc, grad_bdec, loss)


def on_device(acts, enc_weight, dec_weight, enc_bias, dec_bias):
    tok_rows, width = acts.shape
    layer_count = lax.axis_size("layer")
    latent_count = lax.axis_size("latent")
    first_col = lax.axis_index("layer") * width
    col_layer = (first_col + jnp.arange(width, dtype=jnp.int32)) // D
    onehot = (col_layer[:, None] == jnp.arange(LAYERS, dtype=jnp.int32)[None, :]).astype(
        jnp.float32
    )
    dec_wide = dec_weight.astype(jnp.float32)
    part_squares = jnp.dot(dec_wide * dec_wide, onehot, precision=lax.Precision.HIGHEST)
    layer_squares = lax.psum(part_squares, "layer")
    norms = jnp.sqrt(layer_squares + 1e-06)
    weight = jnp.sum(norms, axis=1)
    partial_pre = jnp.dot(acts, enc_weight, preferred_element_type=jnp.float32)
    pre = lax.psum(partial_pre, "layer") + enc_bias
    feats = jnp.maximum(pre, 0.0).astype(jnp.bfloat16)
    active = feats > 0
    partial_recon = jnp.dot(feats, dec_weight, preferred_element_type=jnp.float32)
    recon = lax.psum(partial_recon, "latent") + dec_bias
    error = recon - acts.astype(jnp.float32)
    feats_wide = feats.astype(jnp.float32)
    mse_local = jnp.sum(error * error)
    sparse_local = jnp.sum(feats_wide * weight[None, :])
    totals = lax.psum((mse_local, sparse_local), ("layer", "latent"))
    total = totals[0] / latent_count + 4.0 * totals[1] / layer_count
    loss = (total / (tok_rows * LAYERS * D)).reshape(1)
    grad_error = (2.0 / tok_rows * error).astype(jnp.bfloat16)
    grad_bdec = jnp.sum(grad_error.astype(jnp.float32), axis=0)
    feat_total = jnp.sum(feats_wide, axis=0)
    outer = lax.dot_general(
        feats, grad_error, (((0,), (0,)), ((), ())), preferred_element_type=jnp.float32
    )
    col_norms = jnp.dot(norms, onehot.T, precision=lax.Precision.HIGHEST)
    grad_dec = (outer + 4.0 / tok_rows * feat_total[:, None] * dec_wide / col_norms).astype(
        jnp.bfloat16
    )
    partial_grad = lax.dot_general(
        grad_error, dec_weight, (((1,), (1,)), ((), ())), preferred_element_type=jnp.float32
    )
    penalty = 4.0 / tok_rows * weight[None, :]
    grad_share = lax.psum_scatter(partial_grad, "layer", scatter_dimension=0, tiled=True) + penalty
    share_rows = grad_share.shape[0]
    active_share = lax.dynamic_slice_in_dim(
        active, lax.axis_index("layer") * share_rows, share_rows, 0
    )
    pre_share = jnp.where(active_share, grad_share, 0.0).astype(jnp.bfloat16)
    grad_pre = lax.all_gather(pre_share, "layer", axis=0, tiled=True)
    grad_benc = jnp.sum(grad_pre.astype(jnp.float32), axis=0)
    grad_enc = lax.dot_general(
        acts, grad_pre, (((0,), (0,)), ((), ())), preferred_element_type=jnp.float32
    ).astype(jnp.bfloat16)
    return (grad_enc, grad_dec, grad_benc, grad_bdec, loss)


def solution(mesh):
    placed = (
        P("groups", "layer"),
        P("layer", ("groups", "latent")),
        P(("groups", "latent"), "layer"),
        P(("groups", "latent")),
        P(("groups", "layer")),
    )
    plain = mesh.shape["layer"] != LAYERS or mesh.shape["latent"] != 4
    return jax.shard_map(
        on_device if plain else on_device_kernel,
        mesh=mesh,
        in_specs=placed,
        out_specs=(
            P("layer", ("groups", "latent")),
            P(("groups", "latent"), "layer"),
            P(("groups", "latent")),
            P(("groups", "layer")),
            P("groups"),
        ),
        check_vma=False,
    )
```

```python
import functools

import jax
import jax.numpy as jnp
from jax import lax
from jax.experimental import pallas as pl
from jax.experimental.pallas import tpu as pltpu
from jax.sharding import PartitionSpec as P

D = 3584
LAYERS = 4
PIECE = 128
MESH = pl.DeviceIdType.MESH
F32 = jnp.float32
BF16 = jnp.bfloat16


def tokens_kernel(
    layer_count, acts_h, enc_h, dec_h, ebias, dbias, norms_in,
    feats_h, gerr_h, gpre_h, feat_sum, err_sum, gpre_sum, loss,
    enc_v, dec_v, acts_a, acts_e, part, pre_in, feats, out_half, own_half, core_in, x_in,
    gerr, gpart, g_in, gpre, norms_all,
    mse, wsum, fsum, esum, bsum, lslots, lpair, lin,
    load_sem, acts_sem, acte_sem, store_sem, norm_send, norm_recv,
    ps, pr, fs, fr, cs, cr, xs, xr, es, er, gs, gr, bs, br, ls, lr,
):
    tok_rows, width = acts_h.shape
    lat = enc_h.shape[1]
    T = PIECE
    H = T // 2
    NP = tok_rows // T
    last = layer_count - 1
    grp, z, k = lax.axis_index("groups"), lax.axis_index("layer"), lax.axis_index("latent")
    core = k % 2
    mate = (grp, z, k + 1 - 2 * core)
    across = (grp, z, (k + 2) % 4)

    def level(i):
        return (grp, i, k)

    enc_load = pltpu.make_async_copy(enc_h, enc_v, load_sem.at[0])
    dec_load = pltpu.make_async_copy(dec_h, dec_v, load_sem.at[1])

    def acts_load(p):
        return pltpu.make_async_copy(
            acts_h.at[pl.ds(p * T, T)], acts_a.at[p % 2], acts_sem.at[p % 2]
        )

    def acte_load(p):
        return pltpu.make_async_copy(
            acts_h.at[pl.ds(p * T + core * H, H)], acts_e.at[p % 2], acte_sem.at[p % 2]
        )

    enc_load.start()
    acts_load(0).start()
    dec_load.start()
    for held in (mse, fsum, esum, bsum):
        held[...] = jnp.zeros_like(held)

    barrier = pltpu.get_barrier_semaphore()
    for step in range(1, layer_count):
        pl.semaphore_signal(
            barrier, inc=1, device_id=level((z + step) % layer_count), device_id_type=MESH
        )
    pl.semaphore_signal(barrier, inc=1, device_id=mate, device_id_type=MESH)
    pl.semaphore_signal(barrier, inc=1, device_id=across, device_id_type=MESH)
    pl.semaphore_wait(barrier, layer_count + 1)

    def remote(src, dst, send, recv, dev):
        return pltpu.make_async_remote_copy(
            src_ref=src, dst_ref=dst, send_sem=send, recv_sem=recv,
            device_id=dev, device_id_type=MESH,
        )

    def norm_copy(step):
        return remote(
            norms_in, norms_all.at[step], norm_send.at[step], norm_recv.at[step],
            level((z + step) % layer_count),
        )

    for step in range(1, layer_count):
        norm_copy(step).start()

    def half_rows(way, p):
        return pl.ds(pl.multiple_of(p * T + way * H, H), H)

    def pos_of(way):
        return z if way == 0 else last - z

    def onward(way, by):
        nxt = z + by if way == 0 else z - by
        return level(jnp.clip(nxt, 0, last))

    def pre_copy(way, p):
        return remote(part.at[half_rows(way, p)], pre_in.at[half_rows(way, p)],
                      ps.at[way, p], pr.at[way, p], onward(way, 1))

    def feat_copy(way, p):
        return remote(feats.at[half_rows(way, p)], feats.at[half_rows(way, p)],
                      fs.at[way, p], fr.at[way, p], onward(way, -1))

    def grad_copy(way, p):
        return remote(gpart.at[half_rows(way, p)], g_in.at[half_rows(way, p)],
                      gs.at[way, p], gr.at[way, p], onward(way, 1))

    def gpre_copy(way, p):
        return remote(gpre.at[half_rows(way, p)], gpre.at[half_rows(way, p)],
                      bs.at[way, p], br.at[way, p], onward(way, -1))

    def half_of(p):
        return pl.ds(pl.multiple_of(p * H, H), H)

    def core_copy(p):
        return remote(out_half.at[half_of(p)], core_in.at[half_of(p)], cs.at[p], cr.at[p], mate)

    def x_copy(p):
        return remote(own_half.at[half_of(p)], x_in.at[half_of(p)], xs.at[p], xr.at[p], across)

    def err_copy(p):
        rows = pl.ds(pl.multiple_of(p * T + core * H, H), H)
        return remote(gerr.at[rows], gerr.at[rows], es.at[p], er.at[p], mate)

    def piece_rows(p):
        return pl.ds(pl.multiple_of(p * T, T), T)

    def store(which, p):
        src, dst = ((feats, feats_h), (gerr, gerr_h), (gpre, gpre_h))[which]
        return pltpu.make_async_copy(
            src.at[piece_rows(p)], dst.at[piece_rows(p)], store_sem.at[which, p]
        )

    def valid(p):
        return jnp.logical_and(p >= 0, p < NP)

    def pre_chain(t, first):
        for way in range(2):
            pos = pos_of(way)
            p = t - pos
            here = pos == 0 if first else pos > 0

            @pl.when(jnp.logical_and(valid(p), here))
            def _():
                rows = half_rows(way, p)
                if not first:
                    pre_copy(way, p).wait_recv()

                    @pl.loop(0, lat // 256)
                    def _(n):
                        cols = pl.ds(pl.multiple_of(n * 256, 256), 256)
                        part[rows, cols] += pre_in[rows, cols]

                    @pl.when(pos < last)
                    def _():
                        pre_copy(way, p).start()

                    @pl.when(pos == last)
                    def _():
                        @pl.loop(0, lat // 256)
                        def _(n):
                            cols = pl.ds(pl.multiple_of(n * 256, 256), 256)
                            feats[rows, cols] = jnp.maximum(
                                part[rows, cols] + ebias[:, cols], 0.0
                            ).astype(BF16)
                        feat_copy(way, p).start()
                else:
                    pre_copy(way, p).start()

    def grad_chain(t, first):
        for way in range(2):
            pos = pos_of(way)
            p = t - pos
            here = pos == 0 if first else pos > 0

            @pl.when(jnp.logical_and(valid(p), here))
            def _():
                rows = half_rows(way, p)
                if not first:
                    grad_copy(way, p).wait_recv()

                    @pl.when(pos < last)
                    def _():
                        @pl.loop(0, lat // 256)
                        def _(n):
                            cols = pl.ds(pl.multiple_of(n * 256, 256), 256)
                            gpart[rows, cols] = (
                                gpart[rows, cols].astype(F32) + g_in[rows, cols].astype(F32)
                            ).astype(BF16)
                        grad_copy(way, p).start()

                    @pl.when(pos == last)
                    def _():
                        @pl.loop(0, lat // 256)
                        def _(n):
                            cols = pl.ds(pl.multiple_of(n * 256, 256), 256)
                            total = (
                                gpart[rows, cols].astype(F32)
                                + g_in[rows, cols].astype(F32)
                                + 4.0 / tok_rows * wsum[0:1, cols]
                            )
                            live = feats[rows, cols].astype(F32) > 0.0
                            gpre[rows, cols] = jnp.where(live, total, 0.0).astype(BF16)
                        gpre_copy(way, p).start()
                else:
                    grad_copy(way, p).start()

    def back(t, copy):
        for way in range(2):
            pos = pos_of(way)
            p = t - (2 * last - pos)

            @pl.when(jnp.logical_and(valid(p), pos < last))
            def _():
                copy(way, p).wait_recv()

                @pl.when(pos > 0)
                def _():
                    copy(way, p).start()

    def loss_copy(step):
        return remote(lslots.at[z], lslots.at[z], ls.at[step], lr.at[step],
                      level((z + step) % layer_count))

    def loss_pair(i):
        return remote(lpair.at[i], lin.at[i], ls.at[layer_count + i], lr.at[layer_count + i],
                      (mate, across)[i])

    enc_load.wait()
    LR = 2 * last
    LC, LX, LG = LR + 1, LR + 2, LR + 2

    @pl.loop(0, NP + LG + 2 * last + 1)
    def _(t):
        @pl.when(t == LR)
        def _():
            dec_load.wait()
            total = norms_in[...]
            for step in range(1, layer_count):
                norm_copy(step).wait_recv()
                total = total + norms_all[step]
            wsum[...] = total

        @pl.when(t == NP + LX)
        def _():
            mine = 0.5 * jnp.sum(mse[...]) + 4.0 / layer_count * jnp.sum(
                jnp.sum(fsum[...], axis=0, keepdims=True) * wsum[0:1, :]
            )
            lslots[z] = jnp.full((8, 128), mine, F32)
            for step in range(1, layer_count):
                loss_copy(step).start()

        @pl.when(t == NP + LX + 1)
        def _():
            for step in range(1, layer_count):
                loss_copy(step).wait_recv()
            total = lslots[0]
            for i in range(1, layer_count):
                total = total + lslots[i]
            lpair[0] = total
            loss_pair(0).start()

        @pl.when(t == NP + LX + 2)
        def _():
            loss_pair(0).wait_recv()
            lpair[1] = lpair[0] + lin[0]
            loss_pair(1).start()

        @pl.when(t == NP + LX + 3)
        def _():
            loss_pair(1).wait_recv()
            loss[...] = (lpair[1] + lin[1]) / (tok_rows * LAYERS * D)

        back(t - LG, gpre_copy)
        p_done = t - LG - 2 * last

        @pl.when(valid(p_done))
        def _():
            store(2, p_done).start()
            rows = piece_rows(p_done)

            @pl.loop(0, lat // 256)
            def _(n):
                cols = pl.ds(pl.multiple_of(n * 256, 256), 256)
                bsum[:, cols] += jnp.sum(
                    gpre[rows, cols].astype(F32).reshape(T // 8, 8, 256), axis=0
                )

        grad_chain(t - LG, False)
        back(t, feat_copy)
        pre_chain(t, False)

        p_x = t - LX

        @pl.when(valid(p_x))
        def _():
            x_copy(p_x).wait_recv()
            acte_load(p_x).wait()
            rows = half_of(p_x)
            grows = pl.ds(pl.multiple_of(p_x * T + core * H, H), H)

            @pl.loop(0, width // 256)
            def _(n):
                cols = pl.ds(pl.multiple_of(n * 256, 256), 256)
                error = (
                    own_half[rows, cols].astype(F32) + x_in[rows, cols].astype(F32)
                    + dbias[:, cols] - acts_e[p_x % 2, :, cols].astype(F32)
                )
                mse[:, cols] += jnp.sum((error * error).reshape(H // 8, 8, 256), axis=0)
                gerr[grows, cols] = (2.0 / tok_rows * error).astype(BF16)
            err_copy(p_x).start()

        p_c = t - LC

        @pl.when(valid(p_c))
        def _():
            acte_load(p_c).start()
            core_copy(p_c).wait_recv()
            rows = half_of(p_c)

            @pl.loop(0, width // 256)
            def _(n):
                cols = pl.ds(pl.multiple_of(n * 256, 256), 256)
                own_half[rows, cols] = (
                    own_half[rows, cols].astype(F32) + core_in[rows, cols].astype(F32)
                ).astype(BF16)
            x_copy(p_c).start()

        @pl.when(t < NP)
        def _():
            acts_load(t).wait()

            @pl.when(t + 1 < NP)
            def _():
                acts_load(t + 1).start()

            rows = piece_rows(t)

            @pl.loop(0, lat // 256)
            def _(n):
                cols = pl.ds(pl.multiple_of(n * 256, 256), 256)
                part[rows, cols] = jnp.dot(
                    acts_a[t % 2], enc_v[:, cols], preferred_element_type=F32
                )
        pre_chain(t, True)

        p_r = t - LR

        @pl.when(valid(p_r))
        def _():
            store(0, p_r).start()
            mine = pl.ds(pl.multiple_of(p_r * T + core * H, H), H)
            other = pl.ds(pl.multiple_of(p_r * T + (1 - core) * H, H), H)
            rows = half_of(p_r)
            whole = piece_rows(p_r)

            @pl.loop(0, lat // 256)
            def _(n):
                cols = pl.ds(pl.multiple_of(n * 256, 256), 256)
                fsum[:, cols] += jnp.sum(
                    feats[whole, cols].astype(F32).reshape(T // 8, 8, 256), axis=0
                )

            @pl.loop(0, width // 512)
            def _(n):
                cols = pl.ds(pl.multiple_of(n * 512, 512), 512)
                both = jnp.concatenate([feats[mine, :], feats[other, :]], axis=0)
                made = jnp.dot(both, dec_v[:, cols], preferred_element_type=F32)
                own_half[rows, cols] = made[:H].astype(BF16)
                out_half[rows, cols] = made[H:].astype(BF16)
            core_copy(p_r).start()

        p_g = t - LG

        @pl.when(valid(p_g))
        def _():
            err_copy(p_g).wait_recv()
            store(1, p_g).start()
            rows = piece_rows(p_g)

            @pl.loop(0, lat // 256)
            def _(n):
                cols = pl.ds(pl.multiple_of(n * 256, 256), 256)
                gpart[rows, cols] = lax.dot_general(
                    gerr[rows, :], dec_v[cols, :], (((1,), (1,)), ((), ())),
                    preferred_element_type=F32,
                ).astype(BF16)
        grad_chain(t - LG, True)

        @pl.when(valid(p_g))
        def _():
            rows = piece_rows(p_g)

            @pl.loop(0, width // 256)
            def _(n):
                cols = pl.ds(pl.multiple_of(n * 256, 256), 256)
                esum[:, cols] += jnp.sum(
                    gerr[rows, cols].astype(F32).reshape(T // 8, 8, 256), axis=0
                )

    feat_sum[...] = jnp.sum(fsum[...], axis=0, keepdims=True)
    err_sum[...] = jnp.sum(esum[...], axis=0, keepdims=True)
    gpre_sum[...] = jnp.sum(bsum[...], axis=0, keepdims=True)
    for i in range(2):
        loss_pair(i).wait_send()
    for step in range(1, layer_count):
        loss_copy(step).wait_send()

    for step in range(1, layer_count):
        norm_copy(step).wait_send()

    @pl.loop(0, NP)
    def _(p):
        for which in range(3):
            store(which, p).wait()
        core_copy(p).wait_send()
        x_copy(p).wait_send()
        err_copy(p).wait_send()
        for way in range(2):
            pos = pos_of(way)

            @pl.when(pos < last)
            def _():
                pre_copy(way, p).wait_send()
                grad_copy(way, p).wait_send()

            @pl.when(pos > 0)
            def _():
                feat_copy(way, p).wait_send()
                gpre_copy(way, p).wait_send()


def encoder_kernel(acts, gpre, out):
    out[...] = lax.dot_general(
        acts[...], gpre[...], (((0,), (0,)), ((), ())), preferred_element_type=F32
    ).astype(BF16)


def on_device_kernel(acts, enc_weight, dec_weight, enc_bias, dec_bias):
    tok_rows, width = acts.shape
    lat = enc_weight.shape[1]
    layer_count = lax.axis_size("layer")
    dec_wide = dec_weight.astype(F32)
    norms = jnp.sqrt(jnp.sum(dec_wide * dec_wide, axis=1) + 1e-06)
    half = tok_rows // 2
    pieces = tok_rows // PIECE
    dma = pltpu.SemaphoreType.DMA
    vm = pl.BlockSpec(memory_space=pltpu.VMEM)
    hb = pl.BlockSpec(memory_space=pl.ANY)
    feats, grad_error, grad_pre, feat_total, err_total, gpre_total, loss = pl.pallas_call(
        functools.partial(tokens_kernel, layer_count),
        out_shape=(
            jax.ShapeDtypeStruct((tok_rows, lat), BF16),
            jax.ShapeDtypeStruct((tok_rows, width), BF16),
            jax.ShapeDtypeStruct((tok_rows, lat), BF16),
            jax.ShapeDtypeStruct((1, lat), F32),
            jax.ShapeDtypeStruct((1, width), F32),
            jax.ShapeDtypeStruct((1, lat), F32),
            jax.ShapeDtypeStruct((8, 128), F32),
        ),
        in_specs=[hb, hb, hb, vm, vm, vm],
        out_specs=(hb, hb, hb, vm, vm, vm, vm),
        scratch_shapes=[
            pltpu.VMEM((width, lat), BF16),
            pltpu.VMEM((lat, width), BF16),
            pltpu.VMEM((2, PIECE, width), BF16),
            pltpu.VMEM((2, PIECE // 2, width), BF16),
            pltpu.VMEM((tok_rows, lat), F32),
            pltpu.VMEM((tok_rows, lat), F32),
            pltpu.VMEM((tok_rows, lat), BF16),
            pltpu.VMEM((half, width), BF16),
            pltpu.VMEM((half, width), BF16),
            pltpu.VMEM((half, width), BF16),
            pltpu.VMEM((half, width), BF16),
            pltpu.VMEM((tok_rows, width), BF16),
            pltpu.VMEM((tok_rows, lat), BF16),
            pltpu.VMEM((tok_rows, lat), BF16),
            pltpu.VMEM((tok_rows, lat), BF16),
            pltpu.VMEM((layer_count, 8, lat), F32),
            pltpu.VMEM((8, width), F32),
            pltpu.VMEM((8, lat), F32),
            pltpu.VMEM((8, lat), F32),
            pltpu.VMEM((8, width), F32),
            pltpu.VMEM((8, lat), F32),
            pltpu.VMEM((layer_count, 8, 128), F32),
            pltpu.VMEM((2, 8, 128), F32),
            pltpu.VMEM((2, 8, 128), F32),
            dma((2,)), dma((2,)), dma((2,)), dma((3, pieces)),
            dma((layer_count,)), dma((layer_count,)),
            dma((2, pieces)), dma((2, pieces)), dma((2, pieces)), dma((2, pieces)),
            dma((pieces,)), dma((pieces,)), dma((pieces,)), dma((pieces,)),
            dma((pieces,)), dma((pieces,)),
            dma((2, pieces)), dma((2, pieces)), dma((2, pieces)), dma((2, pieces)),
            dma((layer_count + 2,)), dma((layer_count + 2,)),
        ],
        compiler_params=pltpu.CompilerParams(
            collective_id=0, has_side_effects=True, vmem_limit_bytes=62 * 1024 * 1024
        ),
        cost_estimate=pl.CostEstimate(
            flops=6 * tok_rows * width * lat, bytes_accessed=8 * tok_rows * width, transcendentals=0
        ),
    )(
        acts, enc_weight, dec_weight, enc_bias.reshape(1, lat), dec_bias.reshape(1, width),
        jnp.broadcast_to(norms[None, :], (8, lat)),
    )
    outer = lax.dot_general(
        feats, grad_error, (((0,), (0,)), ((), ())), preferred_element_type=F32
    )
    coef = 4.0 / tok_rows * feat_total[0] / norms
    grad_dec = (outer + coef[:, None] * dec_wide).astype(BF16)
    tile = 512
    grad_enc = pl.pallas_call(
        encoder_kernel,
        grid=(width // tile,),
        out_shape=jax.ShapeDtypeStruct((width, lat), BF16),
        in_specs=[
            pl.BlockSpec((tok_rows, tile), lambda i: (0, i)),
            pl.BlockSpec((tok_rows, lat), lambda i: (0, 0)),
        ],
        out_specs=pl.BlockSpec((tile, lat), lambda i: (i, 0)),
        compiler_params=pltpu.CompilerParams(vmem_limit_bytes=32 * 1024 * 1024),
        cost_estimate=pl.CostEstimate(
            flops=2 * tok_rows * width * lat, bytes_accessed=4 * tok_rows * width, transcendentals=0
        ),
    )(acts, grad_pre)
    return (grad_enc, grad_dec, gpre_total[0], err_total[0], loss[0, 0:1])


def on_device(acts, enc_weight, dec_weight, enc_bias, dec_bias):
    tok_rows, width = acts.shape
    layer_count = lax.axis_size("layer")
    latent_count = lax.axis_size("latent")
    first_col = lax.axis_index("layer") * width
    col_layer = (first_col + jnp.arange(width, dtype=jnp.int32)) // D
    onehot = (col_layer[:, None] == jnp.arange(LAYERS, dtype=jnp.int32)[None, :]).astype(
        jnp.float32
    )
    dec_wide = dec_weight.astype(jnp.float32)
    part_squares = jnp.dot(dec_wide * dec_wide, onehot, precision=lax.Precision.HIGHEST)
    layer_squares = lax.psum(part_squares, "layer")
    norms = jnp.sqrt(layer_squares + 1e-06)
    weight = jnp.sum(norms, axis=1)
    partial_pre = jnp.dot(acts, enc_weight, preferred_element_type=jnp.float32)
    pre = lax.psum(partial_pre, "layer") + enc_bias
    feats = jnp.maximum(pre, 0.0).astype(jnp.bfloat16)
    active = feats > 0
    partial_recon = jnp.dot(feats, dec_weight, preferred_element_type=jnp.float32)
    recon = lax.psum(partial_recon, "latent") + dec_bias
    error = recon - acts.astype(jnp.float32)
    feats_wide = feats.astype(jnp.float32)
    mse_local = jnp.sum(error * error)
    sparse_local = jnp.sum(feats_wide * weight[None, :])
    totals = lax.psum((mse_local, sparse_local), ("layer", "latent"))
    total = totals[0] / latent_count + 4.0 * totals[1] / layer_count
    loss = (total / (tok_rows * LAYERS * D)).reshape(1)
    grad_error = (2.0 / tok_rows * error).astype(jnp.bfloat16)
    grad_bdec = jnp.sum(grad_error.astype(jnp.float32), axis=0)
    feat_total = jnp.sum(feats_wide, axis=0)
    outer = lax.dot_general(
        feats, grad_error, (((0,), (0,)), ((), ())), preferred_element_type=jnp.float32
    )
    col_norms = jnp.dot(norms, onehot.T, precision=lax.Precision.HIGHEST)
    grad_dec = (outer + 4.0 / tok_rows * feat_total[:, None] * dec_wide / col_norms).astype(
        jnp.bfloat16
    )
    partial_grad = lax.dot_general(
        grad_error, dec_weight, (((1,), (1,)), ((), ())), preferred_element_type=jnp.float32
    )
    penalty = 4.0 / tok_rows * weight[None, :]
    grad_share = lax.psum_scatter(partial_grad, "layer", scatter_dimension=0, tiled=True) + penalty
    share_rows = grad_share.shape[0]
    active_share = lax.dynamic_slice_in_dim(
        active, lax.axis_index("layer") * share_rows, share_rows, 0
    )
    pre_share = jnp.where(active_share, grad_share, 0.0).astype(jnp.bfloat16)
    grad_pre = lax.all_gather(pre_share, "layer", axis=0, tiled=True)
    grad_benc = jnp.sum(grad_pre.astype(jnp.float32), axis=0)
    grad_enc = lax.dot_general(
        acts, grad_pre, (((0,), (0,)), ((), ())), preferred_element_type=jnp.float32
    ).astype(jnp.bfloat16)
    return (grad_enc, grad_dec, grad_benc, grad_bdec, loss)


def solution(mesh):
    placed = (
        P("groups", "layer"),
        P("layer", ("groups", "latent")),
        P(("groups", "latent"), "layer"),
        P(("groups", "latent")),
        P(("groups", "layer")),
    )
    plain = mesh.shape["layer"] != LAYERS or mesh.shape["latent"] != 4
    return jax.shard_map(
        on_device if plain else on_device_kernel,
        mesh=mesh,
        in_specs=placed,
        out_specs=(
            P("layer", ("groups", "latent")),
            P(("groups", "latent"), "layer"),
            P(("groups", "latent")),
            P(("groups", "layer")),
            P("groups"),
        ),
        check_vma=False,
    )
```

```python
import functools

import jax
import jax.numpy as jnp
from jax import lax
from jax.experimental import pallas as pl
from jax.experimental.pallas import tpu as pltpu
from jax.sharding import PartitionSpec as P

D = 3584
LAYERS = 4
PIECE = 128
MESH = pl.DeviceIdType.MESH
F32 = jnp.float32
BF16 = jnp.bfloat16


def tokens_kernel(
    layer_count, acts_h, enc_h, dec_h, ebias, dbias, norms_in,
    feats_h, gerr_h, gpre_h, feat_sum, err_sum, gpre_sum, loss,
    enc_v, dec_v, acts_a, acts_e, part, pre_in, feats, out_half, own_half, core_in, x_in,
    gerr, gpart, g_in, gpre, norms_all,
    mse, wsum, fsum, esum, bsum, lslots, lpair, lin,
    load_sem, acts_sem, acte_sem, store_sem, norm_send, norm_recv,
    ps, pr, fs, fr, cs, cr, xs, xr, es, er, gs, gr, bs, br, ls, lr,
):
    tok_rows, width = acts_h.shape
    lat = enc_h.shape[1]
    T = PIECE
    H = T // 2
    NP = tok_rows // T
    last = layer_count - 1
    grp, z, k = lax.axis_index("groups"), lax.axis_index("layer"), lax.axis_index("latent")
    core = k % 2
    mate = (grp, z, k + 1 - 2 * core)
    across = (grp, z, (k + 2) % 4)

    def level(i):
        return (grp, i, k)

    enc_load = pltpu.make_async_copy(enc_h, enc_v, load_sem.at[0])
    dec_load = pltpu.make_async_copy(dec_h, dec_v, load_sem.at[1])

    def acts_load(p):
        return pltpu.make_async_copy(
            acts_h.at[pl.ds(p * T, T)], acts_a.at[p % 2], acts_sem.at[p % 2]
        )

    def acte_load(p):
        return pltpu.make_async_copy(
            acts_h.at[pl.ds(p * T + core * H, H)], acts_e.at[p % 2], acte_sem.at[p % 2]
        )

    enc_load.start()
    acts_load(0).start()
    dec_load.start()
    for held in (mse, fsum, esum, bsum):
        held[...] = jnp.zeros_like(held)

    barrier = pltpu.get_barrier_semaphore()
    for step in range(1, layer_count):
        pl.semaphore_signal(
            barrier, inc=1, device_id=level((z + step) % layer_count), device_id_type=MESH
        )
    pl.semaphore_signal(barrier, inc=1, device_id=mate, device_id_type=MESH)
    pl.semaphore_signal(barrier, inc=1, device_id=across, device_id_type=MESH)
    pl.semaphore_wait(barrier, layer_count + 1)

    def remote(src, dst, send, recv, dev):
        return pltpu.make_async_remote_copy(
            src_ref=src, dst_ref=dst, send_sem=send, recv_sem=recv,
            device_id=dev, device_id_type=MESH,
        )

    def norm_copy(step):
        return remote(
            norms_in, norms_all.at[step], norm_send.at[step], norm_recv.at[step],
            level((z + step) % layer_count),
        )

    for step in range(1, layer_count):
        norm_copy(step).start()

    def half_rows(way, p):
        return pl.ds(pl.multiple_of(p * T + way * H, H), H)

    def pos_of(way):
        return z if way == 0 else last - z

    def onward(way, by):
        nxt = z + by if way == 0 else z - by
        return level(jnp.clip(nxt, 0, last))

    def pre_copy(way, p):
        return remote(part.at[half_rows(way, p)], pre_in.at[half_rows(way, p)],
                      ps.at[way, p], pr.at[way, p], onward(way, 1))

    def feat_copy(way, p):
        return remote(feats.at[half_rows(way, p)], feats.at[half_rows(way, p)],
                      fs.at[way, p], fr.at[way, p], onward(way, -1))

    def grad_copy(way, p):
        return remote(gpart.at[half_rows(way, p)], g_in.at[half_rows(way, p)],
                      gs.at[way, p], gr.at[way, p], onward(way, 1))

    def gpre_copy(way, p):
        return remote(gpre.at[half_rows(way, p)], gpre.at[half_rows(way, p)],
                      bs.at[way, p], br.at[way, p], onward(way, -1))

    def half_of(p):
        return pl.ds(pl.multiple_of(p * H, H), H)

    def core_copy(p):
        return remote(out_half.at[half_of(p)], core_in.at[half_of(p)], cs.at[p], cr.at[p], mate)

    def x_copy(p):
        return remote(own_half.at[half_of(p)], x_in.at[half_of(p)], xs.at[p], xr.at[p], across)

    def err_copy(p):
        rows = pl.ds(pl.multiple_of(p * T + core * H, H), H)
        return remote(gerr.at[rows], gerr.at[rows], es.at[p], er.at[p], mate)

    def piece_rows(p):
        return pl.ds(pl.multiple_of(p * T, T), T)

    def store(which, p):
        src, dst = ((feats, feats_h), (gerr, gerr_h), (gpre, gpre_h))[which]
        return pltpu.make_async_copy(
            src.at[piece_rows(p)], dst.at[piece_rows(p)], store_sem.at[which, p]
        )

    def valid(p):
        return jnp.logical_and(p >= 0, p < NP)

    def pre_chain(t, first):
        for way in range(2):
            pos = pos_of(way)
            p = t - pos
            here = pos == 0 if first else pos > 0

            @pl.when(jnp.logical_and(valid(p), here))
            def _():
                rows = half_rows(way, p)
                if not first:
                    pre_copy(way, p).wait_recv()

                    @pl.loop(0, lat // 256)
                    def _(n):
                        cols = pl.ds(pl.multiple_of(n * 256, 256), 256)
                        part[rows, cols] += pre_in[rows, cols]

                    @pl.when(pos < last)
                    def _():
                        pre_copy(way, p).start()

                    @pl.when(pos == last)
                    def _():
                        @pl.loop(0, lat // 256)
                        def _(n):
                            cols = pl.ds(pl.multiple_of(n * 256, 256), 256)
                            feats[rows, cols] = jnp.maximum(
                                part[rows, cols] + ebias[:, cols], 0.0
                            ).astype(BF16)
                        feat_copy(way, p).start()
                else:
                    pre_copy(way, p).start()

    def grad_chain(t, first):
        for way in range(2):
            pos = pos_of(way)
            p = t - pos
            here = pos == 0 if first else pos > 0

            @pl.when(jnp.logical_and(valid(p), here))
            def _():
                rows = half_rows(way, p)
                if not first:
                    grad_copy(way, p).wait_recv()

                    @pl.when(pos < last)
                    def _():
                        @pl.loop(0, lat // 256)
                        def _(n):
                            cols = pl.ds(pl.multiple_of(n * 256, 256), 256)
                            gpart[rows, cols] = (
                                gpart[rows, cols].astype(F32) + g_in[rows, cols].astype(F32)
                            ).astype(BF16)
                        grad_copy(way, p).start()

                    @pl.when(pos == last)
                    def _():
                        @pl.loop(0, lat // 256)
                        def _(n):
                            cols = pl.ds(pl.multiple_of(n * 256, 256), 256)
                            total = (
                                gpart[rows, cols].astype(F32)
                                + g_in[rows, cols].astype(F32)
                                + 4.0 / tok_rows * wsum[0:1, cols]
                            )
                            live = feats[rows, cols].astype(F32) > 0.0
                            gpre[rows, cols] = jnp.where(live, total, 0.0).astype(BF16)
                        gpre_copy(way, p).start()
                else:
                    grad_copy(way, p).start()

    def back(t, copy):
        for way in range(2):
            pos = pos_of(way)
            p = t - (2 * last - pos)

            @pl.when(jnp.logical_and(valid(p), pos < last))
            def _():
                copy(way, p).wait_recv()

                @pl.when(pos > 0)
                def _():
                    copy(way, p).start()

    def loss_copy(step):
        return remote(lslots.at[z], lslots.at[z], ls.at[step], lr.at[step],
                      level((z + step) % layer_count))

    def loss_pair(i):
        return remote(lpair.at[i], lin.at[i], ls.at[layer_count + i], lr.at[layer_count + i],
                      (mate, across)[i])

    enc_load.wait()
    LR = 2 * last
    LC, LX, LG = LR + 1, LR + 2, LR + 2

    @pl.loop(0, NP + LG + 2 * last + 1)
    def _(t):
        @pl.when(t == LR)
        def _():
            dec_load.wait()
            total = norms_in[...]
            for step in range(1, layer_count):
                norm_copy(step).wait_recv()
                total = total + norms_all[step]
            wsum[...] = total

        @pl.when(t == NP + LX)
        def _():
            mine = 0.5 * jnp.sum(mse[...]) + 4.0 / layer_count * jnp.sum(
                jnp.sum(fsum[...], axis=0, keepdims=True) * wsum[0:1, :]
            )
            lslots[z] = jnp.full((8, 128), mine, F32)
            for step in range(1, layer_count):
                loss_copy(step).start()

        @pl.when(t == NP + LX + 1)
        def _():
            for step in range(1, layer_count):
                loss_copy(step).wait_recv()
            total = lslots[0]
            for i in range(1, layer_count):
                total = total + lslots[i]
            lpair[0] = total
            loss_pair(0).start()

        @pl.when(t == NP + LX + 2)
        def _():
            loss_pair(0).wait_recv()
            lpair[1] = lpair[0] + lin[0]
            loss_pair(1).start()

        @pl.when(t == NP + LX + 3)
        def _():
            loss_pair(1).wait_recv()
            loss[...] = (lpair[1] + lin[1]) / (tok_rows * LAYERS * D)

        back(t - LG, gpre_copy)
        p_done = t - LG - 2 * last

        @pl.when(valid(p_done))
        def _():
            store(2, p_done).start()
            rows = piece_rows(p_done)

            @pl.loop(0, lat // 256)
            def _(n):
                cols = pl.ds(pl.multiple_of(n * 256, 256), 256)
                bsum[:, cols] += jnp.sum(
                    gpre[rows, cols].astype(F32).reshape(T // 8, 8, 256), axis=0
                )

        grad_chain(t - LG, False)
        back(t, feat_copy)
        pre_chain(t, False)

        p_c = t - LC

        @pl.when(valid(p_c))
        def _():
            acte_load(p_c).start()
            core_copy(p_c).wait_recv()
            rows = half_of(p_c)

            @pl.loop(0, width // 256)
            def _(n):
                cols = pl.ds(pl.multiple_of(n * 256, 256), 256)
                own_half[rows, cols] = (
                    own_half[rows, cols].astype(F32) + core_in[rows, cols].astype(F32)
                ).astype(BF16)
            x_copy(p_c).start()

        p_x = t - LX

        @pl.when(valid(p_x))
        def _():
            x_copy(p_x).wait_recv()
            acte_load(p_x).wait()
            rows = half_of(p_x)
            grows = pl.ds(pl.multiple_of(p_x * T + core * H, H), H)

            @pl.loop(0, width // 256)
            def _(n):
                cols = pl.ds(pl.multiple_of(n * 256, 256), 256)
                error = (
                    own_half[rows, cols].astype(F32) + x_in[rows, cols].astype(F32)
                    + dbias[:, cols] - acts_e[p_x % 2, :, cols].astype(F32)
                )
                mse[:, cols] += jnp.sum((error * error).reshape(H // 8, 8, 256), axis=0)
                gerr[grows, cols] = (2.0 / tok_rows * error).astype(BF16)
            err_copy(p_x).start()

        @pl.when(t < NP)
        def _():
            acts_load(t).wait()

            @pl.when(t + 1 < NP)
            def _():
                acts_load(t + 1).start()

            rows = piece_rows(t)

            @pl.loop(0, lat // 512)
            def _(n):
                cols = pl.ds(pl.multiple_of(n * 512, 512), 512)
                part[rows, cols] = jnp.dot(
                    acts_a[t % 2], enc_v[:, cols], preferred_element_type=F32
                )
        pre_chain(t, True)

        p_r = t - LR

        @pl.when(valid(p_r))
        def _():
            store(0, p_r).start()
            mine = pl.ds(pl.multiple_of(p_r * T + core * H, H), H)
            other = pl.ds(pl.multiple_of(p_r * T + (1 - core) * H, H), H)
            rows = half_of(p_r)
            whole = piece_rows(p_r)

            @pl.loop(0, lat // 256)
            def _(n):
                cols = pl.ds(pl.multiple_of(n * 256, 256), 256)
                fsum[:, cols] += jnp.sum(
                    feats[whole, cols].astype(F32).reshape(T // 8, 8, 256), axis=0
                )

            @pl.loop(0, width // 512)
            def _(n):
                cols = pl.ds(pl.multiple_of(n * 512, 512), 512)
                both = jnp.concatenate([feats[mine, :], feats[other, :]], axis=0)
                made = jnp.dot(both, dec_v[:, cols], preferred_element_type=F32)
                own_half[rows, cols] = made[:H].astype(BF16)
                out_half[rows, cols] = made[H:].astype(BF16)
            core_copy(p_r).start()

        p_g = t - LG

        @pl.when(valid(p_g))
        def _():
            err_copy(p_g).wait_recv()
            store(1, p_g).start()
            rows = piece_rows(p_g)

            @pl.loop(0, lat // 512)
            def _(n):
                cols = pl.ds(pl.multiple_of(n * 512, 512), 512)
                gpart[rows, cols] = lax.dot_general(
                    gerr[rows, :], dec_v[cols, :], (((1,), (1,)), ((), ())),
                    preferred_element_type=F32,
                ).astype(BF16)
        grad_chain(t - LG, True)

        @pl.when(valid(p_g))
        def _():
            rows = piece_rows(p_g)

            @pl.loop(0, width // 256)
            def _(n):
                cols = pl.ds(pl.multiple_of(n * 256, 256), 256)
                esum[:, cols] += jnp.sum(
                    gerr[rows, cols].astype(F32).reshape(T // 8, 8, 256), axis=0
                )

    feat_sum[...] = jnp.sum(fsum[...], axis=0, keepdims=True)
    err_sum[...] = jnp.sum(esum[...], axis=0, keepdims=True)
    gpre_sum[...] = jnp.sum(bsum[...], axis=0, keepdims=True)
    for i in range(2):
        loss_pair(i).wait_send()
    for step in range(1, layer_count):
        loss_copy(step).wait_send()

    for step in range(1, layer_count):
        norm_copy(step).wait_send()

    @pl.loop(0, NP)
    def _(p):
        for which in range(3):
            store(which, p).wait()
        core_copy(p).wait_send()
        x_copy(p).wait_send()
        err_copy(p).wait_send()
        for way in range(2):
            pos = pos_of(way)

            @pl.when(pos < last)
            def _():
                pre_copy(way, p).wait_send()
                grad_copy(way, p).wait_send()

            @pl.when(pos > 0)
            def _():
                feat_copy(way, p).wait_send()
                gpre_copy(way, p).wait_send()


def encoder_kernel(acts, gpre, out):
    out[...] = lax.dot_general(
        acts[...], gpre[...], (((0,), (0,)), ((), ())), preferred_element_type=F32
    ).astype(BF16)


def on_device_kernel(acts, enc_weight, dec_weight, enc_bias, dec_bias):
    tok_rows, width = acts.shape
    lat = enc_weight.shape[1]
    layer_count = lax.axis_size("layer")
    dec_wide = dec_weight.astype(F32)
    norms = jnp.sqrt(jnp.sum(dec_wide * dec_wide, axis=1) + 1e-06)
    half = tok_rows // 2
    pieces = tok_rows // PIECE
    dma = pltpu.SemaphoreType.DMA
    vm = pl.BlockSpec(memory_space=pltpu.VMEM)
    hb = pl.BlockSpec(memory_space=pl.ANY)
    feats, grad_error, grad_pre, feat_total, err_total, gpre_total, loss = pl.pallas_call(
        functools.partial(tokens_kernel, layer_count),
        out_shape=(
            jax.ShapeDtypeStruct((tok_rows, lat), BF16),
            jax.ShapeDtypeStruct((tok_rows, width), BF16),
            jax.ShapeDtypeStruct((tok_rows, lat), BF16),
            jax.ShapeDtypeStruct((1, lat), F32),
            jax.ShapeDtypeStruct((1, width), F32),
            jax.ShapeDtypeStruct((1, lat), F32),
            jax.ShapeDtypeStruct((8, 128), F32),
        ),
        in_specs=[hb, hb, hb, vm, vm, vm],
        out_specs=(hb, hb, hb, vm, vm, vm, vm),
        scratch_shapes=[
            pltpu.VMEM((width, lat), BF16),
            pltpu.VMEM((lat, width), BF16),
            pltpu.VMEM((2, PIECE, width), BF16),
            pltpu.VMEM((2, PIECE // 2, width), BF16),
            pltpu.VMEM((tok_rows, lat), F32),
            pltpu.VMEM((tok_rows, lat), F32),
            pltpu.VMEM((tok_rows, lat), BF16),
            pltpu.VMEM((half, width), BF16),
            pltpu.VMEM((half, width), BF16),
            pltpu.VMEM((half, width), BF16),
            pltpu.VMEM((half, width), BF16),
            pltpu.VMEM((tok_rows, width), BF16),
            pltpu.VMEM((tok_rows, lat), BF16),
            pltpu.VMEM((tok_rows, lat), BF16),
            pltpu.VMEM((tok_rows, lat), BF16),
            pltpu.VMEM((layer_count, 8, lat), F32),
            pltpu.VMEM((8, width), F32),
            pltpu.VMEM((8, lat), F32),
            pltpu.VMEM((8, lat), F32),
            pltpu.VMEM((8, width), F32),
            pltpu.VMEM((8, lat), F32),
            pltpu.VMEM((layer_count, 8, 128), F32),
            pltpu.VMEM((2, 8, 128), F32),
            pltpu.VMEM((2, 8, 128), F32),
            dma((2,)), dma((2,)), dma((2,)), dma((3, pieces)),
            dma((layer_count,)), dma((layer_count,)),
            dma((2, pieces)), dma((2, pieces)), dma((2, pieces)), dma((2, pieces)),
            dma((pieces,)), dma((pieces,)), dma((pieces,)), dma((pieces,)),
            dma((pieces,)), dma((pieces,)),
            dma((2, pieces)), dma((2, pieces)), dma((2, pieces)), dma((2, pieces)),
            dma((layer_count + 2,)), dma((layer_count + 2,)),
        ],
        compiler_params=pltpu.CompilerParams(
            collective_id=0, has_side_effects=True, vmem_limit_bytes=62 * 1024 * 1024
        ),
        cost_estimate=pl.CostEstimate(
            flops=6 * tok_rows * width * lat, bytes_accessed=8 * tok_rows * width, transcendentals=0
        ),
    )(
        acts, enc_weight, dec_weight, enc_bias.reshape(1, lat), dec_bias.reshape(1, width),
        jnp.broadcast_to(norms[None, :], (8, lat)),
    )
    outer = lax.dot_general(
        feats, grad_error, (((0,), (0,)), ((), ())), preferred_element_type=F32
    )
    coef = 4.0 / tok_rows * feat_total[0] / norms
    grad_dec = (outer + coef[:, None] * dec_wide).astype(BF16)
    tile = 512
    grad_enc = pl.pallas_call(
        encoder_kernel,
        grid=(width // tile,),
        out_shape=jax.ShapeDtypeStruct((width, lat), BF16),
        in_specs=[
            pl.BlockSpec((tok_rows, tile), lambda i: (0, i)),
            pl.BlockSpec((tok_rows, lat), lambda i: (0, 0)),
        ],
        out_specs=pl.BlockSpec((tile, lat), lambda i: (i, 0)),
        compiler_params=pltpu.CompilerParams(vmem_limit_bytes=32 * 1024 * 1024),
        cost_estimate=pl.CostEstimate(
            flops=2 * tok_rows * width * lat, bytes_accessed=4 * tok_rows * width, transcendentals=0
        ),
    )(acts, grad_pre)
    return (grad_enc, grad_dec, gpre_total[0], err_total[0], loss[0, 0:1])


def on_device(acts, enc_weight, dec_weight, enc_bias, dec_bias):
    tok_rows, width = acts.shape
    layer_count = lax.axis_size("layer")
    latent_count = lax.axis_size("latent")
    first_col = lax.axis_index("layer") * width
    col_layer = (first_col + jnp.arange(width, dtype=jnp.int32)) // D
    onehot = (col_layer[:, None] == jnp.arange(LAYERS, dtype=jnp.int32)[None, :]).astype(
        jnp.float32
    )
    dec_wide = dec_weight.astype(jnp.float32)
    part_squares = jnp.dot(dec_wide * dec_wide, onehot, precision=lax.Precision.HIGHEST)
    layer_squares = lax.psum(part_squares, "layer")
    norms = jnp.sqrt(layer_squares + 1e-06)
    weight = jnp.sum(norms, axis=1)
    partial_pre = jnp.dot(acts, enc_weight, preferred_element_type=jnp.float32)
    pre = lax.psum(partial_pre, "layer") + enc_bias
    feats = jnp.maximum(pre, 0.0).astype(jnp.bfloat16)
    active = feats > 0
    partial_recon = jnp.dot(feats, dec_weight, preferred_element_type=jnp.float32)
    recon = lax.psum(partial_recon, "latent") + dec_bias
    error = recon - acts.astype(jnp.float32)
    feats_wide = feats.astype(jnp.float32)
    mse_local = jnp.sum(error * error)
    sparse_local = jnp.sum(feats_wide * weight[None, :])
    totals = lax.psum((mse_local, sparse_local), ("layer", "latent"))
    total = totals[0] / latent_count + 4.0 * totals[1] / layer_count
    loss = (total / (tok_rows * LAYERS * D)).reshape(1)
    grad_error = (2.0 / tok_rows * error).astype(jnp.bfloat16)
    grad_bdec = jnp.sum(grad_error.astype(jnp.float32), axis=0)
    feat_total = jnp.sum(feats_wide, axis=0)
    outer = lax.dot_general(
        feats, grad_error, (((0,), (0,)), ((), ())), preferred_element_type=jnp.float32
    )
    col_norms = jnp.dot(norms, onehot.T, precision=lax.Precision.HIGHEST)
    grad_dec = (outer + 4.0 / tok_rows * feat_total[:, None] * dec_wide / col_norms).astype(
        jnp.bfloat16
    )
    partial_grad = lax.dot_general(
        grad_error, dec_weight, (((1,), (1,)), ((), ())), preferred_element_type=jnp.float32
    )
    penalty = 4.0 / tok_rows * weight[None, :]
    grad_share = lax.psum_scatter(partial_grad, "layer", scatter_dimension=0, tiled=True) + penalty
    share_rows = grad_share.shape[0]
    active_share = lax.dynamic_slice_in_dim(
        active, lax.axis_index("layer") * share_rows, share_rows, 0
    )
    pre_share = jnp.where(active_share, grad_share, 0.0).astype(jnp.bfloat16)
    grad_pre = lax.all_gather(pre_share, "layer", axis=0, tiled=True)
    grad_benc = jnp.sum(grad_pre.astype(jnp.float32), axis=0)
    grad_enc = lax.dot_general(
        acts, grad_pre, (((0,), (0,)), ((), ())), preferred_element_type=jnp.float32
    ).astype(jnp.bfloat16)
    return (grad_enc, grad_dec, grad_benc, grad_bdec, loss)


def solution(mesh):
    placed = (
        P("groups", "layer"),
        P("layer", ("groups", "latent")),
        P(("groups", "latent"), "layer"),
        P(("groups", "latent")),
        P(("groups", "layer")),
    )
    plain = mesh.shape["layer"] != LAYERS or mesh.shape["latent"] != 4
    return jax.shard_map(
        on_device if plain else on_device_kernel,
        mesh=mesh,
        in_specs=placed,
        out_specs=(
            P("layer", ("groups", "latent")),
            P(("groups", "latent"), "layer"),
            P(("groups", "latent")),
            P(("groups", "layer")),
            P("groups"),
        ),
        check_vma=False,
    )
```
